32 devices in a mesh: aa: 4 (over x, core), ba: 4 (over z), col: 2 (over y).
Axes of the slice: x: 2, y: 2, z: 4, core: 2. Of those that a mesh axis runs over, the one named last changes fastest.
Arguments:
- inputs: float32 [64, 128, 32, 128], P('aa', 'ba', 'col'), may hold values from -6 to 6
- cotangent: float32 [64, 128, 32, 128], P('aa', 'ba', 'col'), may hold values from -6 to 6
- w_gate: float32 [128, 128], replicated, may hold values from -0.5 to 0.5
- w_value: float32 [128, 128], replicated, may hold values from -0.5 to 0.5
- mix_first: float32 [64, 64], replicated, may hold values from -0.75 to 0.75
- mix_second: float32 [128, 128], replicated, may hold values from -0.5 to 0.5
- mix_third: float32 [32, 32], replicated, may hold values from -1 to 1
- twiddle_first: float32 [64, 128, 32], P('aa', 'ba', 'col'), may hold values from 0.4 to 1.6
- twiddle_second: float32 [64, 128, 32], P('aa', 'ba', 'col'), may hold values from 0.4 to 1.6
- twiddle_third: float32 [64, 128, 32], P('aa', 'ba', 'col'), may hold values from 0.4 to 1.6
Outputs:
- output: float32 [64, 128, 32, 128], P('aa', 'ba', 'col')
- grad_inputs: float32 [64, 128, 32, 128], P('aa', 'ba', 'col')
- grad_gate: float32 [128, 128], replicated
- grad_value: float32 [128, 128], replicated
- grad_first: float32 [64, 64], replicated
- grad_second: float32 [128, 128], replicated
- grad_third: float32 [32, 32], replicated
The draws below stay inside these ranges and needn't reach their ends.
All inputs are finite; a program needn't handle non-finite values.
Results may differ from the reference program's by a relative error of at most 0.00016.
Values sent between devices are 32-bit elements; how exact they have to be, the bound alone decides.
A program may use at most 192 MiB of HBM per device.

```python
import jax
import jax.numpy as jnp
from jax import lax

DIG1 = 64
DIG2 = 128
DIG3 = 32
CH = 128
SEQ = 262144


def shard_levels(stream_key, shape, cuts, least, largest):
    factor_of = 1.0
    for dim, parts in cuts:
        heights = jax.random.uniform(jax.random.fold_in(jax.random.fold_in(stream_key, 6), dim), (parts,), jnp.float32, least / len(cuts), largest / len(cuts))
        factor_of = factor_of * jnp.repeat(jnp.exp(heights), shape[dim] // parts).reshape((-1,) + (1,) * (len(shape) - 1 - dim))
    return factor_of


def centred(key, dims, spread, most, pieces=(), dtype=jnp.bfloat16):
    drawn = spread * jax.random.normal(key, dims, jnp.float32)
    if pieces:
        drawn = drawn * shard_levels(key, dims, pieces, -0.22, 0.18)
    return jnp.clip(drawn, -most, most).astype(dtype)


def setup_inputs(seed: int = 0) -> dict:
    streams_of = jax.random.split(jax.random.key(seed), 11)
    return {
        "inputs": centred(streams_of[0], (DIG1, DIG2, DIG3, CH), 1.0, 6.0, ((0, 4), (1, 4), (2, 2)), jnp.float32),
        "cotangent": centred(streams_of[1], (DIG1, DIG2, DIG3, CH), 1.0, 6.0, ((0, 4), (1, 4), (2, 2)), jnp.float32),
        "w_gate": centred(streams_of[2], (CH, CH), CH ** -0.5, 0.5, (), jnp.float32),
        "w_value": centred(streams_of[3], (CH, CH), CH ** -0.5, 0.5, (), jnp.float32),
        "mix_first": centred(streams_of[4], (DIG1, DIG1), DIG1 ** -0.5, 0.75, (), jnp.float32),
        "mix_second": centred(streams_of[5], (DIG2, DIG2), DIG2 ** -0.5, 0.5, (), jnp.float32),
        "mix_third": centred(streams_of[6], (DIG3, DIG3), DIG3 ** -0.5, 1.0, (), jnp.float32),
        "twiddle_first": jnp.clip(0.4 + 1.2 * jax.random.uniform(streams_of[7], (DIG1, DIG2, DIG3), jnp.float32) ** shard_levels(streams_of[7], (DIG1, DIG2, DIG3), ((0, 4), (1, 4), (2, 2)), -0.2, 0.2), 0.4, 1.6),
        "twiddle_second": jnp.clip(0.4 + 1.2 * jax.random.uniform(streams_of[8], (DIG1, DIG2, DIG3), jnp.float32) ** shard_levels(streams_of[8], (DIG1, DIG2, DIG3), ((0, 4), (1, 4), (2, 2)), -0.2, 0.2), 0.4, 1.6),
        "twiddle_third": jnp.clip(0.4 + 1.2 * jax.random.uniform(streams_of[9], (DIG1, DIG2, DIG3), jnp.float32) ** shard_levels(streams_of[9], (DIG1, DIG2, DIG3), ((0, 4), (1, 4), (2, 2)), -0.2, 0.2), 0.4, 1.6),
    }


def reference(inputs, cotangent, w_gate, w_value, mix_first, mix_second, mix_third, twiddle_first, twiddle_second, twiddle_third):
    highest = lax.Precision.HIGHEST
    gate = jnp.einsum('ijkc,cd->ijkd', inputs, w_gate, precision=highest)
    value = jnp.einsum('ijkc,cd->ijkd', inputs, w_value, precision=highest)
    sigmoid_gate = jax.nn.sigmoid(gate)
    grad_mixed = cotangent * sigmoid_gate
    block_width = min(16, CH)
    mixed_parts = []
    grad_parts = []
    raw_first = jnp.zeros((DIG1, DIG1), jnp.float32)
    raw_second = jnp.zeros((DIG2, DIG2), jnp.float32)
    raw_third = jnp.zeros((DIG3, DIG3), jnp.float32)
    for block_index in range(CH // block_width):
        low = block_index * block_width
        value_block = value[..., low:low + block_width]
        upstream = grad_mixed[..., low:low + block_width]
        first_in = twiddle_first[..., None] * value_block
        first_out = jnp.einsum('xi,ijkc->xjkc', mix_first, first_in, precision=highest)
        second_in = twiddle_second[..., None] * first_out
        second_out = jnp.einsum('yj,ijkc->iykc', mix_second, second_in, precision=highest)
        third_in = twiddle_third[..., None] * second_out
        mixed_parts.append(jnp.einsum('zk,ijkc->ijzc', mix_third, third_in, precision=highest))
        grad_third_in = jnp.einsum('zk,ijzc->ijkc', mix_third, upstream, precision=highest)
        raw_third = raw_third + jnp.einsum('ijzc,ijkc->zk', upstream, third_in, precision=highest)
        grad_second_out = twiddle_third[..., None] * grad_third_in
        grad_second_in = jnp.einsum('yj,iykc->ijkc', mix_second, grad_second_out, precision=highest)
        raw_second = raw_second + jnp.einsum('iykc,ijkc->yj', grad_second_out, second_in, precision=highest)
        grad_first_out = twiddle_second[..., None] * grad_second_in
        grad_first_in = jnp.einsum('xi,xjkc->ijkc', mix_first, grad_first_out, precision=highest)
        raw_first = raw_first + jnp.einsum('xjkc,ijkc->xi', grad_first_out, first_in, precision=highest)
        grad_parts.append(twiddle_first[..., None] * grad_first_in)
    mixed = jnp.concatenate(mixed_parts, axis=3)
    grad_value_act = jnp.concatenate(grad_parts, axis=3)
    output = sigmoid_gate * mixed
    grad_gate_act = cotangent * mixed * sigmoid_gate * (1.0 - sigmoid_gate)
    grad_inputs = jnp.einsum('ijkd,cd->ijkc', grad_gate_act, w_gate, precision=highest) + jnp.einsum('ijkd,cd->ijkc', grad_value_act, w_value, precision=highest)
    raw_gate = jnp.einsum('ijkc,ijkd->cd', inputs, grad_gate_act, precision=highest)
    raw_value = jnp.einsum('ijkc,ijkd->cd', inputs, grad_value_act, precision=highest)
    factor = float(SEQ) ** -0.5
    return (output, grad_inputs, raw_gate * factor, raw_value * factor, raw_first * factor, raw_second * factor, raw_third * factor)
```

```python
import functools

import jax
import jax.numpy as jnp
from jax import lax
from jax.experimental import pallas as pl
from jax.experimental.pallas import tpu as pltpu
from jax.sharding import PartitionSpec as P

F32 = jnp.float32
BF16 = jnp.bfloat16
MESH = pl.DeviceIdType.MESH
VMEM = pltpu.VMEM
LIMIT = 56 * 1024 * 1024
SUB = 8


def split(x):
    hi = x.astype(BF16)
    return hi, (x - hi.astype(F32)).astype(BF16)


def split_weight(x):
    hi = lax.reduce_precision(x, 8, 7)
    return hi.astype(BF16), (x - hi).astype(BF16)


def dot(a, b, dims=((1,), (0,))):
    return lax.dot_general(a, b, (dims, ((), ())), preferred_element_type=F32)


def dot3(a, b, dims=((1,), (0,))):
    return dot(a[0], b[0], dims) + (dot(a[0], b[1], dims) + dot(a[1], b[0], dims))


NT = ((1,), (1,))
TN = ((0,), (0,))


def expand(m, inner):
    n = m.shape[0]
    row = lax.broadcasted_iota(jnp.int32, (n * SUB, n * SUB), 0)
    col = lax.broadcasted_iota(jnp.int32, (n * SUB, n * SUB), 1)
    at = lax.broadcasted_iota(jnp.int32, (n * SUB, n), 0)
    place = at // SUB if inner else at % n
    pick = (place == lax.broadcasted_iota(jnp.int32, (n * SUB, n), 1)).astype(F32)
    highest = lax.Precision.HIGHEST
    spread = jnp.dot(jnp.dot(pick, m, precision=highest), pick.T, precision=highest)
    kept = row % SUB == col % SUB if inner else row // n == col // n
    return jnp.where(kept, spread, 0.0)


def coords():
    return {n: lax.axis_index(n) for n in ("aa", "ba", "col")}


def sizes():
    return {n: lax.axis_size(n) for n in ("aa", "ba", "col")}


def peers(axes, size):
    me = coords()
    total = 1
    mine = 0
    for n in axes:
        mine = mine * size[n] + me[n]
        total *= size[n]
    found = []
    for step in range(total):
        at = lax.rem(mine + step, total)
        there = dict(me)
        for n in reversed(axes):
            there[n] = lax.rem(at, size[n])
            at = at // size[n]
        found.append(there)
    return found


def barrier(groups, size):
    sem = pltpu.get_barrier_semaphore()
    count = 0
    for axes, skip in groups:
        for step, there in enumerate(peers(axes, size)):
            if step == 0 or (skip is not None and skip(step)):
                continue
            pl.semaphore_signal(sem, inc=1, device_id=there, device_id_type=MESH)
            count += 1
    pl.semaphore_wait(sem, count)


def send(axes, size, source, target, send_sem, recv_sem):
    me = coords()
    copies = []
    for step, there in enumerate(peers(axes, size)):
        if step == 0:
            copy = pltpu.make_async_copy(source(there), target(me), send_sem.at[0])
        else:
            copy = pltpu.make_async_remote_copy(
                src_ref=source(there),
                dst_ref=target(me),
                send_sem=send_sem.at[step],
                recv_sem=recv_sem.at[step],
                device_id=there,
                device_id_type=MESH,
            )
        copy.start()
        copies.append(copy)
    return copies


def finish(*groups):
    for copies in groups:
        for copy in copies:
            copy.wait()


def block(index, width):
    return pl.ds(pl.multiple_of(index * width, width), width)


def lanes(parts):
    return parts[0] if len(parts) == 1 else jnp.concatenate(parts, axis=1)


def gather_first(ref, j):
    n, _, k, c = ref.shape
    return lanes([ref[:, j, t * SUB:(t + 1) * SUB, :].reshape(n * SUB, c) for t in range(k // SUB)])


def scatter_first(ref, j, value):
    n, _, k, c = ref.shape
    for t in range(k // SUB):
        ref[:, j, t * SUB:(t + 1) * SUB, :] = value[:, t * c:(t + 1) * c].reshape(n, SUB, c)


def gather_second(ref, i):
    _, n, k, c = ref.shape
    return lanes([ref[i, :, t * SUB:(t + 1) * SUB, :].reshape(n * SUB, c) for t in range(k // SUB)])


def scatter_second(ref, i, value):
    _, n, k, c = ref.shape
    for t in range(k // SUB):
        ref[i, :, t * SUB:(t + 1) * SUB, :] = value[:, t * c:(t + 1) * c].reshape(n, SUB, c)


def gather_third(ref, i):
    _, r, k, c = ref.shape
    return lanes([ref[i, t * SUB:(t + 1) * SUB, :, :].reshape(SUB * k, c) for t in range(r // SUB)])


def scatter_third(ref, i, value):
    _, r, k, c = ref.shape
    for t in range(r // SUB):
        ref[i, t * SUB:(t + 1) * SUB, :, :] = value[:, t * c:(t + 1) * c].reshape(SUB, k, c)


def loop(count, body):
    def step(i, carry):
        body(i)
        return carry

    lax.fori_loop(0, count, step, 0)


def fold_inner(p, n):
    rows = lax.broadcasted_iota(jnp.int32, p.shape, 0)
    cols = lax.broadcasted_iota(jnp.int32, p.shape, 1)
    kept = jnp.where(lax.rem(rows, SUB) == lax.rem(cols, SUB), p, 0.0)
    summed = jnp.sum(kept.reshape(n, SUB, n * SUB), axis=1)
    pick = (
        lax.broadcasted_iota(jnp.int32, (n * SUB, n), 0) // SUB
        == lax.broadcasted_iota(jnp.int32, (n * SUB, n), 1)
    ).astype(F32)
    return jnp.dot(summed, pick, precision=lax.Precision.HIGHEST, preferred_element_type=F32)


def fold_outer(p, n):
    rows = lax.broadcasted_iota(jnp.int32, p.shape, 0)
    cols = lax.broadcasted_iota(jnp.int32, p.shape, 1)
    kept = jnp.where(rows // n == cols // n, p, 0.0)
    summed = jnp.sum(kept.reshape(SUB, n, n * SUB), axis=0)
    pick = (
        lax.rem(lax.broadcasted_iota(jnp.int32, (n * SUB, n), 0), n)
        == lax.broadcasted_iota(jnp.int32, (n * SUB, n), 1)
    ).astype(F32)
    return jnp.dot(summed, pick, precision=lax.Precision.HIGHEST, preferred_element_type=F32)


def kernel_one(size, x_ref, cot_ref, wh_ref, wl_ref, tw1_ref, tw2_ref, tw3_ref,
               f1_ref, g3_ref, sig_ref, t2_ref, t3_ref, s_buf, g_buf,
               sa, ra, sc, rc, s2, r2, s3, r3):
    h1, h2, h3, c = x_ref.shape
    q = f1_ref.shape[1]
    r = g3_ref.shape[1]
    barrier([(("aa",), None), (("ba",), None), (("col",), None)], size)
    tw2 = send(("aa",), size, lambda t: tw2_ref.at[t["aa"]], lambda m: t2_ref.at[m["aa"]], s2, r2)
    tw3 = send(("ba",), size, lambda t: tw3_ref.at[t["ba"]], lambda m: t3_ref.at[m["ba"]], s3, r3)

    def work(i):
        both = dot3(split(x_ref[i].reshape(h2 * h3, c)), (wh_ref[...], wl_ref[...]))
        sig = jax.nn.sigmoid(both[:, :c]).reshape(h2, h3, c)
        sig_ref[i] = sig
        g_buf[i] = cot_ref[i] * sig
        s_buf[i] = tw1_ref[i] * both[:, c:].reshape(h2, h3, c)

    loop(h1, work)
    first = send(("aa",), size, lambda t: s_buf.at[:, block(t["aa"], q)],
                 lambda m: f1_ref.at[block(m["aa"], h1)], sa, ra)
    third = send(("col",), size, lambda t: g_buf.at[:, block(t["col"], r)],
                 lambda m: g3_ref.at[:, :, block(m["col"], h3), :], sc, rc)
    finish(tw2, tw3, first, third)


def greet(size):
    sem = pltpu.get_barrier_semaphore()
    me = coords()
    count = 0
    for there in peers(("aa", "ba"), size)[1:]:
        pl.semaphore_signal(sem, inc=1, device_id=there, device_id_type=MESH)
        count += 1
    for step in range(1, size["col"]):
        col = lax.rem(me["col"] + step, size["col"])
        for other in range(size["ba"]):
            there = {"aa": me["aa"], "ba": lax.rem(me["ba"] + other, size["ba"]), "col": col}
            pl.semaphore_signal(sem, inc=1, device_id=there, device_id_type=MESH)
            count += 1
    pl.semaphore_wait(sem, count)


def kernel_two(size, f1_ref, g3_ref, m1h, m1l, m3h, m3l, tw2_ref, f2_ref, g2_ref,
               s_buf, g_buf, sa, ra, sb, rb):
    n1, q, h3, c = f1_ref.shape
    h1, r, n3, _ = g3_ref.shape
    p = f2_ref.shape[0]
    h2 = r * size["col"]
    greet(size)

    def mix_first(j):
        out = dot3((m1h[...], m1l[...]), split(gather_first(f1_ref, j)))
        scatter_first(s_buf, j, out * gather_first(tw2_ref, j))

    loop(q, mix_first)
    fwd = send(("aa", "ba"), size, lambda t: s_buf.at[block(t["aa"] * size["ba"] + t["ba"], p)],
               lambda m: f2_ref.at[:, block(m["ba"] * size["aa"] + m["aa"], q)], sa, ra)

    def back_third(i):
        scatter_third(g_buf, i, dot3((m3h[...], m3l[...]), split(gather_third(g3_ref, i))))

    loop(h1, back_third)
    bwd = send(("ba", "col"), size,
               lambda t: g_buf.at[block(t["ba"], p), :, block(t["col"], h3), :],
               lambda m: g2_ref.at[:, block(m["ba"] * size["col"] + m["col"], r)], sb, rb)
    finish(fwd, bwd)


def kernel_three(size, f2_ref, g2_ref, m2h, m2l, m2th, m2tl, tw3_ref, f3_ref, g1_ref, raw_ref,
                 s_buf, g_buf, acc, sa, ra, sb, rb):
    p, n2, h3, c = f2_ref.shape
    r = f3_ref.shape[1]
    q = g1_ref.shape[1]
    h2 = r * size["col"]
    greet(size)

    def mix_second(i):
        out = dot3((m2h[...], m2l[...]), split(gather_second(f2_ref, i)))
        scatter_second(s_buf, i, out * gather_second(tw3_ref, i))

    loop(p, mix_second)
    fwd = send(("ba", "col"), size,
               lambda t: s_buf.at[:, block(t["ba"] * size["col"] + t["col"], r)],
               lambda m: f3_ref.at[block(m["ba"], p), :, block(m["col"], h3), :], sb, rb)

    def back_second(i):
        grad = gather_second(tw3_ref, i) * gather_second(g2_ref, i)
        scatter_second(g_buf, i, dot3((m2th[...], m2tl[...]), split(grad)))

    loop(p, back_second)
    bwd = send(("aa", "ba"), size,
               lambda t: g_buf.at[:, block(t["ba"] * size["aa"] + t["aa"], q)],
               lambda m: g1_ref.at[block(m["aa"] * size["ba"] + m["ba"], p)], sa, ra)

    acc[...] = jnp.zeros_like(acc)

    def raw(i):
        ahead = split(gather_second(f2_ref, i))
        grad = split(gather_second(tw3_ref, i) * gather_second(g2_ref, i))
        for s in range(0, n2 * SUB, 128):
            acc[s:s + 128, :] += dot3((grad[0][s:s + 128], grad[1][s:s + 128]), ahead, NT)

    loop(p, raw)
    raw_ref[...] = fold_inner(acc[...], n2)
    finish(fwd, bwd)


def kernel_four(size, f3_ref, g1_ref, f1_ref, g3_ref, m3h, m3l, m1h, m1l, tw2_ref,
                mixed_ref, g0_ref, raw1_ref, raw3_ref, s_buf, g_buf, acc1, acc3,
                sa, ra, sb, rb):
    h1, r, n3, c = f3_ref.shape
    n1, q, h3, _ = f1_ref.shape
    barrier([(("aa",), None), (("col",), None)], size)

    def mix_third(i):
        scatter_third(s_buf, i, dot3((m3h[...], m3l[...]), split(gather_third(f3_ref, i))))

    loop(h1, mix_third)
    fwd = send(("col",), size, lambda t: s_buf.at[:, :, block(t["col"], h3), :],
               lambda m: mixed_ref.at[:, block(m["col"], r)], sb, rb)

    def back_first(j):
        grad = gather_first(tw2_ref, j) * gather_first(g1_ref, j)
        scatter_first(g_buf, j, dot3((m1h[...], m1l[...]), split(grad)))

    loop(q, back_first)
    bwd = send(("aa",), size, lambda t: g_buf.at[block(t["aa"], h1)],
               lambda m: g0_ref.at[:, block(m["aa"], q)], sa, ra)

    acc1[...] = jnp.zeros_like(acc1)
    acc3[...] = jnp.zeros_like(acc3)

    def raw_first(j):
        ahead = split(gather_first(f1_ref, j))
        grad = split(gather_first(tw2_ref, j) * gather_first(g1_ref, j))
        for s in range(0, n1 * SUB, 128):
            acc1[s:s + 128, :] += dot3((grad[0][s:s + 128], grad[1][s:s + 128]), ahead, NT)

    loop(q, raw_first)

    def raw_third(i):
        acc3[...] += dot3(split(gather_third(g3_ref, i)), split(gather_third(f3_ref, i)), NT)

    loop(h1, raw_third)
    raw1_ref[...] = fold_inner(acc1[...], n1)
    raw3_ref[...] = fold_outer(acc3[...], n3)
    finish(fwd, bwd)


def kernel_five(x_ref, cot_ref, sig_ref, mixed_ref, g0_ref, tw1_ref, wh_ref, wl_ref,
                out_ref, gin_ref, rg_ref, rv_ref):
    _, h2, h3, c = x_ref.shape
    rows = h2 * h3

    @pl.when(pl.program_id(0) == 0)
    def _():
        rg_ref[...] = jnp.zeros_like(rg_ref)
        rv_ref[...] = jnp.zeros_like(rv_ref)

    sig = sig_ref[0].reshape(rows, c)
    out = sig * mixed_ref[0].reshape(rows, c)
    out_ref[0] = out.reshape(h2, h3, c)
    gate = cot_ref[0].reshape(rows, c) * out * (1.0 - sig)
    value = tw1_ref[0].reshape(rows, c) * g0_ref[0].reshape(rows, c)
    both = split(jnp.concatenate([gate, value], axis=1))
    gin = dot3(both, (wh_ref[...], wl_ref[...]), NT)
    gin_ref[0] = gin.reshape(h2, h3, c)
    raw = dot3(split(x_ref[0].reshape(rows, c)), both, TN)
    rg_ref[...] += raw[:, :c]
    rv_ref[...] += raw[:, c:]


def kernel_sum(size, factor, part_ref, out_ref, land, total, sa, ra, sb, rb):
    axes = ("aa", "ba", "col")
    n, ch, _ = part_ref.shape
    barrier([(axes, None)], size)

    def index(t):
        return (t["aa"] * size["ba"] + t["ba"]) * size["col"] + t["col"]

    finish(send(axes, size, lambda t: part_ref.at[index(t)], lambda m: land.at[index(m)], sa, ra))
    total[...] = jnp.sum(land[...], axis=0) * factor
    finish(send(axes, size, lambda t: total, lambda m: out_ref.at[index(m)], sb, rb))


def sems(*counts):
    return [pltpu.SemaphoreType.DMA((n,)) for n in counts for _ in range(2)]


def on_device(inputs, cotangent, w_gate, w_value, mix_first, mix_second, mix_third,
              twiddle_first, twiddle_second, twiddle_third):
    size = sizes()
    na, nb, nc = size["aa"], size["ba"], size["col"]
    h1, h2, h3, c = inputs.shape
    n1, n2, n3 = mix_first.shape[0], mix_second.shape[0], mix_third.shape[0]
    p, q, r = n1 // (na * nb), n2 // (na * nb), h2 // nc
    any_ = pl.BlockSpec(memory_space=pl.ANY)
    vm = pl.BlockSpec(memory_space=VMEM)
    sds = lambda *s: jax.ShapeDtypeStruct(s, F32)
    home, l1, l2, l3 = (h1, h2, h3, c), (n1, q, h3, c), (p, n2, h3, c), (h1, r, n3, c)

    def call(body, cid, outs, out_specs, in_specs, scratch, *args):
        return pl.pallas_call(
            body,
            out_shape=outs,
            in_specs=in_specs,
            out_specs=out_specs,
            scratch_shapes=scratch,
            compiler_params=pltpu.CompilerParams(
                collective_id=cid, has_side_effects=True, vmem_limit_bytes=LIMIT
            ),
        )(*args)

    wide = lambda t: jnp.broadcast_to(t[..., None], t.shape + (c,))
    k1 = split_weight(expand(mix_first, True))
    k1t = split_weight(expand(mix_first.T, True))
    k2 = split_weight(expand(mix_second, True))
    k2t = split_weight(expand(mix_second.T, True))
    k3 = split_weight(expand(mix_third, False))
    k3t = split_weight(expand(mix_third.T, False))
    w = split_weight(jnp.concatenate([w_gate, w_value], axis=1))
    tw1 = wide(twiddle_first)
    tw2s = twiddle_second.reshape(h1, na, q * h3).transpose(1, 0, 2)
    tw3s = twiddle_third.reshape(nb, p, h2 * h3)

    f1, g3, sig, t2, t3 = call(
        functools.partial(kernel_one, size), 0,
        (sds(*l1), sds(*l3), sds(*home), sds(na, h1, q * h3), sds(nb, p, h2 * h3)),
        (any_, any_, vm, any_, any_), [vm] * 5 + [any_] * 2,
        [VMEM(home, F32), VMEM(home, F32)] + sems(na, nc, na, nb),
        inputs, cotangent, *w, tw1, tw2s, tw3s)
    tw2 = wide(t2.reshape(n1, q, h3))
    tw3 = wide(t3.reshape(nb, p, h2, h3).transpose(1, 0, 2, 3).reshape(p, n2, h3))

    f2, g2 = call(
        functools.partial(kernel_two, size), 1, (sds(*l2), sds(*l2)), (any_, any_), [vm] * 7,
        [VMEM(l1, F32), VMEM(l3, F32)] + sems(na * nb, nb * nc),
        f1, g3, *k1, *k3t, tw2)

    f3, g1, raw2 = call(
        functools.partial(kernel_three, size), 2, (sds(*l3), sds(*l1), sds(n2, n2)),
        (any_, any_, vm), [vm] * 7,
        [VMEM(l2, F32), VMEM(l2, F32), VMEM((n2 * SUB, n2 * SUB), F32)] + sems(na * nb, nb * nc),
        f2, g2, *k2, *k2t, tw3)

    mixed, g0, raw1, raw3 = call(
        functools.partial(kernel_four, size), 3,
        (sds(*home), sds(*home), sds(n1, n1), sds(n3, n3)),
        (any_, any_, vm, vm), [vm] * 9,
        [VMEM(l3, F32), VMEM(l1, F32), VMEM((n1 * SUB, n1 * SUB), F32),
         VMEM((n3 * SUB, n3 * SUB), F32)] + sems(na, nc),
        f3, g1, f1, g3, *k3, *k1t, tw2)

    row = pl.BlockSpec((1, h2, h3, c), lambda i: (i, 0, 0, 0))
    whole = lambda *s: pl.BlockSpec(s, lambda i: (0,) * len(s))
    output, grad_inputs, raw_gate, raw_value = pl.pallas_call(
        kernel_five,
        grid=(h1,),
        out_shape=(sds(*home), sds(*home), sds(c, c), sds(c, c)),
        in_specs=[row] * 6 + [whole(c, 2 * c)] * 2,
        out_specs=(row, row, whole(c, c), whole(c, c)),
        compiler_params=pltpu.CompilerParams(vmem_limit_bytes=LIMIT),
    )(inputs, cotangent, sig, mixed, g0, tw1, *w)

    flat = jnp.concatenate([t.reshape(-1) for t in (raw_gate, raw_value, raw2, raw1, raw3)])
    n = na * nb * nc
    unit = n * SUB * 128
    padded = -(-flat.shape[0] // unit) * unit
    parts = jnp.pad(flat, (0, padded - flat.shape[0])).reshape(n, -1, 128)
    factor = float(n1 * n2 * n3) ** (-0.5)
    summed = call(
        functools.partial(kernel_sum, size, factor), 4, sds(*parts.shape), vm, [vm],
        [VMEM(parts.shape, F32), VMEM(parts.shape[1:], F32)] + sems(n, n), parts).reshape(-1)
    at = 0
    order = ((c, c), (c, c), (n2, n2), (n1, n1), (n3, n3))
    taken = []
    for shape in order:
        span = shape[0] * shape[1]
        taken.append(summed[at:at + span].reshape(shape))
        at += span
    return output, grad_inputs, taken[0], taken[1], taken[3], taken[2], taken[4]


def solution(mesh):
    cut = P("aa", "ba", "col", None)
    narrow = P("aa", "ba", "col")
    return jax.shard_map(
        on_device,
        mesh=mesh,
        in_specs=(cut, cut, P(), P(), P(), P(), P(), narrow, narrow, narrow),
        out_specs=(cut, cut, P(), P(), P(), P(), P()),
        check_vma=False,
    )
```

```python
import functools

import jax
import jax.numpy as jnp
from jax import lax
from jax.experimental import pallas as pl
from jax.experimental.pallas import tpu as pltpu
from jax.sharding import PartitionSpec as P

F32 = jnp.float32
BF16 = jnp.bfloat16
MESH = pl.DeviceIdType.MESH
VMEM = pltpu.VMEM
LIMIT = 60 * 1024 * 1024
SUB = 8


def split(x):
    hi = x.astype(BF16)
    return hi, (x - hi.astype(F32)).astype(BF16)


def split_weight(x):
    hi = lax.reduce_precision(x, 8, 7)
    return hi.astype(BF16), (x - hi).astype(BF16)


def dot(a, b, dims=((1,), (0,))):
    return lax.dot_general(a, b, (dims, ((), ())), preferred_element_type=F32)


def dot3(a, b, dims=((1,), (0,))):
    return dot(a[0], b[0], dims) + (dot(a[0], b[1], dims) + dot(a[1], b[0], dims))


NT = ((1,), (1,))
TN = ((0,), (0,))


def expand(m, inner):
    n = m.shape[0]
    row = lax.broadcasted_iota(jnp.int32, (n * SUB, n * SUB), 0)
    col = lax.broadcasted_iota(jnp.int32, (n * SUB, n * SUB), 1)
    at = lax.broadcasted_iota(jnp.int32, (n * SUB, n), 0)
    place = at // SUB if inner else at % n
    pick = (place == lax.broadcasted_iota(jnp.int32, (n * SUB, n), 1)).astype(F32)
    highest = lax.Precision.HIGHEST
    spread = jnp.dot(jnp.dot(pick, m, precision=highest), pick.T, precision=highest)
    kept = row % SUB == col % SUB if inner else row // n == col // n
    return jnp.where(kept, spread, 0.0)


def coords():
    return {n: lax.axis_index(n) for n in ("aa", "ba", "col")}


def sizes():
    return {n: lax.axis_size(n) for n in ("aa", "ba", "col")}


def peers(axes, size):
    me = coords()
    total = 1
    mine = 0
    for n in axes:
        mine = mine * size[n] + me[n]
        total *= size[n]
    found = []
    for step in range(total):
        at = lax.rem(mine + step, total)
        there = dict(me)
        for n in reversed(axes):
            there[n] = lax.rem(at, size[n])
            at = at // size[n]
        found.append(there)
    return found


def barrier(groups, size):
    sem = pltpu.get_barrier_semaphore()
    count = 0
    for axes, skip in groups:
        for step, there in enumerate(peers(axes, size)):
            if step == 0 or (skip is not None and skip(step)):
                continue
            pl.semaphore_signal(sem, inc=1, device_id=there, device_id_type=MESH)
            count += 1
    pl.semaphore_wait(sem, count)


def send(axes, size, source, target, send_sem, recv_sem):
    me = coords()
    copies = []
    for step, there in enumerate(peers(axes, size)):
        if step == 0:
            copy = pltpu.make_async_copy(source(there), target(me), send_sem.at[0])
        else:
            copy = pltpu.make_async_remote_copy(
                src_ref=source(there),
                dst_ref=target(me),
                send_sem=send_sem.at[step],
                recv_sem=recv_sem.at[step],
                device_id=there,
                device_id_type=MESH,
            )
        copy.start()
        copies.append(copy)
    return copies


def finish(*groups):
    for copies in groups:
        for copy in copies:
            copy.wait()


def block(index, width):
    return pl.ds(pl.multiple_of(index * width, width), width)


def lanes(parts):
    return parts[0] if len(parts) == 1 else jnp.concatenate(parts, axis=1)


def gather_second(ref, i):
    _, n, k, c = ref.shape
    return lanes([ref[i, :, t * SUB:(t + 1) * SUB, :].reshape(n * SUB, c) for t in range(k // SUB)])


def gather_third(ref, i):
    _, r, k, c = ref.shape
    return lanes([ref[i, t * SUB:(t + 1) * SUB, :, :].reshape(SUB * k, c) for t in range(r // SUB)])


def scatter_third(ref, i, value):
    _, r, k, c = ref.shape
    for t in range(r // SUB):
        ref[i, t * SUB:(t + 1) * SUB, :, :] = value[:, t * c:(t + 1) * c].reshape(SUB, k, c)


def loop(count, body):
    def step(i, carry):
        body(i)
        return carry

    lax.fori_loop(0, count, step, 0)


def fold_inner(p, n):
    rows = lax.broadcasted_iota(jnp.int32, p.shape, 0)
    cols = lax.broadcasted_iota(jnp.int32, p.shape, 1)
    kept = jnp.where(lax.rem(rows, SUB) == lax.rem(cols, SUB), p, 0.0)
    summed = jnp.sum(kept.reshape(n, SUB, n * SUB), axis=1)
    pick = (
        lax.broadcasted_iota(jnp.int32, (n * SUB, n), 0) // SUB
        == lax.broadcasted_iota(jnp.int32, (n * SUB, n), 1)
    ).astype(F32)
    return jnp.dot(summed, pick, precision=lax.Precision.HIGHEST, preferred_element_type=F32)


def fold_outer(p, n):
    rows = lax.broadcasted_iota(jnp.int32, p.shape, 0)
    cols = lax.broadcasted_iota(jnp.int32, p.shape, 1)
    kept = jnp.where(rows // n == cols // n, p, 0.0)
    summed = jnp.sum(kept.reshape(SUB, n, n * SUB), axis=0)
    pick = (
        lax.rem(lax.broadcasted_iota(jnp.int32, (n * SUB, n), 0), n)
        == lax.broadcasted_iota(jnp.int32, (n * SUB, n), 1)
    ).astype(F32)
    return jnp.dot(summed, pick, precision=lax.Precision.HIGHEST, preferred_element_type=F32)


def kernel_one(size, x_ref, cot_ref, wh_ref, wl_ref, tw1_ref, tw2_ref, tw3_ref,
               first_ref, grad_ref, sig_ref, t2_ref, t3_ref, s2, r2, s3, r3):
    h1, h2, h3, c = x_ref.shape
    barrier([(("aa",), None), (("ba",), None)], size)
    tw2 = send(("aa",), size, lambda t: tw2_ref.at[t["aa"]], lambda m: t2_ref.at[m["aa"]], s2, r2)
    tw3 = send(("ba",), size, lambda t: tw3_ref.at[t["ba"]], lambda m: t3_ref.at[m["ba"]], s3, r3)

    def work(i):
        both = dot3(split(x_ref[i].reshape(h2 * h3, c)), (wh_ref[...], wl_ref[...]))
        sig = jax.nn.sigmoid(both[:, :c]).reshape(h2, h3, c)
        sig_ref[i] = sig
        grad_ref[i] = cot_ref[i] * sig
        first_ref[i] = tw1_ref[i] * both[:, c:].reshape(h2, h3, c)

    loop(h1, work)
    finish(tw2, tw3)


def greet(size):
    sem = pltpu.get_barrier_semaphore()
    me = coords()
    count = 0
    for there in peers(("aa", "ba"), size)[1:]:
        pl.semaphore_signal(sem, inc=1, device_id=there, device_id_type=MESH)
        count += 1
    for step in range(1, size["col"]):
        col = lax.rem(me["col"] + step, size["col"])
        for other in range(size["ba"]):
            there = {"aa": me["aa"], "ba": lax.rem(me["ba"] + other, size["ba"]), "col": col}
            pl.semaphore_signal(sem, inc=1, device_id=there, device_id_type=MESH)
            count += 1
    pl.semaphore_wait(sem, count)


def part(k):
    return slice(k * SUB, (k + 1) * SUB)


def pairs(count):
    return 2 if count % 2 == 0 else 1


def kernel_main(size, first_ref, grad_ref, m1h, m1l, m1th, m1tl, m2h, m2l, m3h, m3l, m3th, m3tl,
                tw2_ref, tw3_ref,
                f1, f2, f3, g3, g2, g1, mixed_ref, g0_ref, raw1_ref, raw2_ref, raw3_ref,
                wf1, wg1, wf2, wg2, wf3, wg3, s_l1, s_l2, g_l2, g_l3, acc1, acc2, acc3, load_sem,
                sa1, ra1, sa2, ra2, sa3, ra3, sa4, ra4, sb4, rb4, sb3, rb3, sb2, rb2, sb1, rb1):
    n1, q, h3, c = f1.shape
    p, n2, _, _ = f2.shape
    h1, r, n3, _ = f3.shape
    na, nb, nc = size["aa"], size["ba"], size["col"]
    steps = range(h3 // SUB)
    half = wf3.shape[0]
    greet(size)

    def load(source, target):
        copy = pltpu.make_async_copy(source, target, load_sem)
        copy.start()
        copy.wait()

    def take_l1(ref, j, k):
        return lanes([ref[:, j + t, k, :].reshape(n1 * SUB, c) for t in range(pairs(q))])

    def put_l1(ref, j, k, value):
        for t in range(pairs(q)):
            ref[:, j + t, k, :] = value[:, t * c:(t + 1) * c].reshape(n1, SUB, c)

    def take_l2(ref, i, k):
        return lanes([ref[i + t, :, k, :].reshape(n2 * SUB, c) for t in range(pairs(p))])

    def put_l2(ref, i, k, value):
        for t in range(pairs(p)):
            ref[i + t, :, k, :] = value[:, t * c:(t + 1) * c].reshape(n2, SUB, c)

    t1 = [
        send(("aa",), size, lambda t: first_ref.at[:, block(t["aa"], q), part(k), :],
             lambda m: f1.at[block(m["aa"], h1), :, part(k), :], sa1.at[k], ra1.at[k])
        for k in steps
    ]
    b4 = send(("col",), size, lambda t: grad_ref.at[:, block(t["col"], r)],
              lambda m: g3.at[:, :, block(m["col"], h3), :], sb4, rb4)

    t2 = []
    for k in steps:
        finish(t1[k])
        load(f1.at[:, :, part(k), :], wf1)

        def mix_first(i):
            j = i * pairs(q)
            out = dot3((m1h[...], m1l[...]), split(take_l1(wf1, j, part(0))))
            put_l1(s_l1, j, part(k), out * take_l1(tw2_ref, j, part(k)))

        loop(q // pairs(q), mix_first)
        t2.append(send(("aa", "ba"), size,
                       lambda t: s_l1.at[block(t["aa"] * nb + t["ba"], p), :, part(k), :],
                       lambda m: f2.at[:, block(m["ba"] * na + m["aa"], q), part(k), :],
                       sa2.at[k], ra2.at[k]))

    finish(b4)
    for h in range(h1 // half):
        load(g3.at[h * half:(h + 1) * half], wg3)

        def back_third(i):
            out = dot3((m3th[...], m3tl[...]), split(gather_third(wg3, i)))
            scatter_third(g_l3, h * half + i, out)

        loop(half, back_third)
    b3 = [
        send(("ba", "col"), size,
             lambda t: g_l3.at[block(t["ba"], p), :, pl.ds(pl.multiple_of(t["col"] * h3 + k * SUB, SUB), SUB), :],
             lambda m: g2.at[:, block(m["ba"] * nc + m["col"], r), part(k), :],
             sb3.at[k], rb3.at[k])
        for k in steps
    ]

    t3 = []
    for k in steps:
        finish(t2[k])
        load(f2.at[:, :, part(k), :], wf2.at[:, :, part(k), :])

        def mix_second(i):
            j = i * pairs(p)
            out = dot3((m2h[...], m2l[...]), split(take_l2(wf2, j, part(k))))
            put_l2(s_l2, j, part(k), out * take_l2(tw3_ref, j, part(k)))

        loop(p // pairs(p), mix_second)
        t3.append(send(("ba", "col"), size,
                       lambda t: s_l2.at[:, block(t["ba"] * nc + t["col"], r), part(k), :],
                       lambda m: f3.at[block(m["ba"], p), :, pl.ds(pl.multiple_of(m["col"] * h3 + k * SUB, SUB), SUB), :],
                       sa3.at[k], ra3.at[k]))

    b2 = []
    for k in steps:
        finish(b3[k])
        load(g2.at[:, :, part(k), :], wg2.at[:, :, part(k), :])

        def back_second(i):
            j = i * pairs(p)
            grad = take_l2(tw3_ref, j, part(k)) * take_l2(wg2, j, part(k))
            put_l2(wg2, j, part(k), grad)
            put_l2(g_l2, j, part(k), dot3((m2h[...], m2l[...]), split(grad), TN))

        loop(p // pairs(p), back_second)
        b2.append(send(("aa", "ba"), size,
                       lambda t: g_l2.at[:, block(t["ba"] * na + t["aa"], q), part(k), :],
                       lambda m: g1.at[block(m["aa"] * nb + m["ba"], p), :, part(k), :],
                       sb2.at[k], rb2.at[k]))

    acc2[...] = jnp.zeros_like(acc2)

    def raw_second(i):
        ahead = split(gather_second(wf2, i))
        grad = split(gather_second(wg2, i))
        for s in range(0, n2 * SUB, 128):
            acc2[s:s + 128, :] += dot3((grad[0][s:s + 128], grad[1][s:s + 128]), ahead, NT)

    loop(p, raw_second)
    raw2_ref[...] = fold_inner(acc2[...], n2)

    finish(*t3)
    for h in range(h1 // half):
        load(f3.at[h * half:(h + 1) * half], wf3)

        def mix_third(i):
            out = dot3((m3h[...], m3l[...]), split(gather_third(wf3, i)))
            scatter_third(g_l3, h * half + i, out)

        loop(half, mix_third)
    t4 = send(("col",), size, lambda t: g_l3.at[:, :, block(t["col"], h3), :],
              lambda m: mixed_ref.at[:, block(m["col"], r)], sa4, ra4)

    acc3[...] = jnp.zeros_like(acc3)
    for h in range(h1 // half):
        load(f3.at[h * half:(h + 1) * half], wf3)
        load(g3.at[h * half:(h + 1) * half], wg3)

        def raw_third(i):
            acc3[...] += dot3(split(gather_third(wg3, i)), split(gather_third(wf3, i)), NT)

        loop(half, raw_third)
    raw3_ref[...] = fold_outer(acc3[...], n3)

    acc1[...] = jnp.zeros_like(acc1)
    b1 = []
    for k in steps:
        finish(b2[k])
        load(g1.at[:, :, part(k), :], wg1)

        def back_first(i):
            j = i * pairs(q)
            grad = take_l1(tw2_ref, j, part(k)) * take_l1(wg1, j, part(0))
            put_l1(wg1, j, part(0), grad)
            put_l1(s_l1, j, part(k), dot3((m1th[...], m1tl[...]), split(grad)))

        loop(q // pairs(q), back_first)
        b1.append(send(("aa",), size, lambda t: s_l1.at[block(t["aa"], h1), :, part(k), :],
                       lambda m: g0_ref.at[:, block(m["aa"], q), part(k), :],
                       sb1.at[k], rb1.at[k]))
        load(f1.at[:, :, part(k), :], wf1)

        def raw_first(i):
            j = i * pairs(q)
            ahead = split(take_l1(wf1, j, part(0)))
            grad = split(take_l1(wg1, j, part(0)))
            for s in range(0, n1 * SUB, 128):
                acc1[s:s + 128, :] += dot3((grad[0][s:s + 128], grad[1][s:s + 128]), ahead, NT)

        loop(q // pairs(q), raw_first)
    raw1_ref[...] = fold_inner(acc1[...], n1)
    finish(t4, *b1)


def kernel_five(x_ref, cot_ref, sig_ref, mixed_ref, g0_ref, tw1_ref, wh_ref, wl_ref,
                out_ref, gin_ref, rg_ref, rv_ref):
    _, h2, h3, c = x_ref.shape
    rows = h2 * h3

    @pl.when(pl.program_id(0) == 0)
    def _():
        rg_ref[...] = jnp.zeros_like(rg_ref)
        rv_ref[...] = jnp.zeros_like(rv_ref)

    sig = sig_ref[0].reshape(rows, c)
    out = sig * mixed_ref[0].reshape(rows, c)
    out_ref[0] = out.reshape(h2, h3, c)
    gate = cot_ref[0].reshape(rows, c) * out * (1.0 - sig)
    value = tw1_ref[0].reshape(rows, c) * g0_ref[0].reshape(rows, c)
    both = split(jnp.concatenate([gate, value], axis=1))
    gin = dot3(both, (wh_ref[...], wl_ref[...]), NT)
    gin_ref[0] = gin.reshape(h2, h3, c)
    raw = dot3(split(x_ref[0].reshape(rows, c)), both, TN)
    rg_ref[...] += raw[:, :c]
    rv_ref[...] += raw[:, c:]


def kernel_sum(size, factor, part_ref, out_ref, land, total, sa, ra, sb, rb):
    axes = ("aa", "ba", "col")
    n, ch, _ = part_ref.shape
    barrier([(axes, None)], size)

    def index(t):
        return (t["aa"] * size["ba"] + t["ba"]) * size["col"] + t["col"]

    finish(send(axes, size, lambda t: part_ref.at[index(t)], lambda m: land.at[index(m)], sa, ra))
    total[...] = jnp.sum(land[...], axis=0) * factor
    finish(send(axes, size, lambda t: total, lambda m: out_ref.at[index(m)], sb, rb))


def sems(*counts):
    shapes = [n if isinstance(n, tuple) else (n,) for n in counts]
    return [pltpu.SemaphoreType.DMA(n) for n in shapes for _ in range(2)]


def on_device(inputs, cotangent, w_gate, w_value, mix_first, mix_second, mix_third,
              twiddle_first, twiddle_second, twiddle_third):
    size = sizes()
    na, nb, nc = size["aa"], size["ba"], size["col"]
    h1, h2, h3, c = inputs.shape
    n1, n2, n3 = mix_first.shape[0], mix_second.shape[0], mix_third.shape[0]
    p, q, r = n1 // (na * nb), n2 // (na * nb), h2 // nc
    any_ = pl.BlockSpec(memory_space=pl.ANY)
    vm = pl.BlockSpec(memory_space=VMEM)
    sds = lambda *s: jax.ShapeDtypeStruct(s, F32)
    home, l1, l2, l3 = (h1, h2, h3, c), (n1, q, h3, c), (p, n2, h3, c), (h1, r, n3, c)

    def call(body, cid, outs, out_specs, in_specs, scratch, *args):
        return pl.pallas_call(
            body,
            out_shape=outs,
            in_specs=in_specs,
            out_specs=out_specs,
            scratch_shapes=scratch,
            compiler_params=pltpu.CompilerParams(
                collective_id=cid, has_side_effects=True, vmem_limit_bytes=LIMIT
            ),
        )(*args)

    wide = lambda t: jnp.broadcast_to(t[..., None], t.shape + (c,))
    k1 = split_weight(expand(mix_first, True))
    k1t = split_weight(expand(mix_first.T, True))
    k2 = split_weight(expand(mix_second, True))
    k3 = split_weight(expand(mix_third, False))
    k3t = split_weight(expand(mix_third.T, False))
    w = split_weight(jnp.concatenate([w_gate, w_value], axis=1))
    tw1 = wide(twiddle_first)
    tw2s = twiddle_second.reshape(h1, na, q * h3).transpose(1, 0, 2)
    tw3s = twiddle_third.reshape(nb, p, h2 * h3)

    first, grad, sig, t2, t3 = call(
        functools.partial(kernel_one, size), 0,
        (sds(*home), sds(*home), sds(*home), sds(na, h1, q * h3), sds(nb, p, h2 * h3)),
        (vm, vm, vm, any_, any_), [vm] * 5 + [any_] * 2, sems(na, nb),
        inputs, cotangent, *w, tw1, tw2s, tw3s)
    tw2 = wide(t2.reshape(n1, q, h3))
    tw3 = wide(t3.reshape(nb, p, h2, h3).transpose(1, 0, 2, 3).reshape(p, n2, h3))

    nk = h3 // SUB
    half = max(h1 // 2, 1)
    *_, mixed, g0, raw1, raw2, raw3 = call(
        functools.partial(kernel_main, size), 1,
        (sds(*l1), sds(*l2), sds(*l3), sds(*l3), sds(*l2), sds(*l1), sds(*home), sds(*home),
         sds(n1, n1), sds(n2, n2), sds(n3, n3)),
        (any_,) * 8 + (vm,) * 3,
        [any_] * 2 + [vm] * 12,
        [VMEM((n1, q, SUB, c), F32)] * 2 + [VMEM(l2, F32)] * 2 + [VMEM((half, r, n3, c), F32)] * 2
        + [VMEM(l1, F32), VMEM(l2, F32), VMEM(l2, F32), VMEM(l3, F32)]
        + [VMEM((n * SUB, n * SUB), F32) for n in (n1, n2, n3)]
        + [pltpu.SemaphoreType.DMA(())]
        + sems((nk, na), (nk, na * nb), (nk, nb * nc), nc, nc, (nk, nb * nc), (nk, na * nb), (nk, na)),
        first, grad, *k1, *k1t, *k2, *k3, *k3t, tw2, tw3)

    row = pl.BlockSpec((1, h2, h3, c), lambda i: (i, 0, 0, 0))
    whole = lambda *s: pl.BlockSpec(s, lambda i: (0,) * len(s))
    output, grad_inputs, raw_gate, raw_value = pl.pallas_call(
        kernel_five,
        grid=(h1,),
        out_shape=(sds(*home), sds(*home), sds(c, c), sds(c, c)),
        in_specs=[row] * 6 + [whole(c, 2 * c)] * 2,
        out_specs=(row, row, whole(c, c), whole(c, c)),
        compiler_params=pltpu.CompilerParams(vmem_limit_bytes=LIMIT),
    )(inputs, cotangent, sig, mixed, g0, tw1, *w)

    flat = jnp.concatenate([t.reshape(-1) for t in (raw_gate, raw_value, raw2, raw1, raw3)])
    n = na * nb * nc
    unit = n * SUB * 128
    padded = -(-flat.shape[0] // unit) * unit
    parts = jnp.pad(flat, (0, padded - flat.shape[0])).reshape(n, -1, 128)
    factor = float(n1 * n2 * n3) ** (-0.5)
    summed = call(
        functools.partial(kernel_sum, size, factor), 2, sds(*parts.shape), vm, [vm],
        [VMEM(parts.shape, F32), VMEM(parts.shape[1:], F32)] + sems(n, n), parts).reshape(-1)
    at = 0
    order = ((c, c), (c, c), (n2, n2), (n1, n1), (n3, n3))
    taken = []
    for shape in order:
        span = shape[0] * shape[1]
        taken.append(summed[at:at + span].reshape(shape))
        at += span
    return output, grad_inputs, taken[0], taken[1], taken[3], taken[2], taken[4]


def solution(mesh):
    cut = P("aa", "ba", "col", None)
    narrow = P("aa", "ba", "col")
    return jax.shard_map(
        on_device,
        mesh=mesh,
        in_specs=(cut, cut, P(), P(), P(), P(), P(), narrow, narrow, narrow),
        out_specs=(cut, cut, P(), P(), P(), P(), P()),
        check_vma=False,
    )
```
